32 devices in a mesh: rows: 8 (over z, y), freq: 4 (over x, core).
Axes of the slice: x: 2, y: 2, z: 4, core: 2. Of those that a mesh axis runs over, the one named last changes fastest.
Arguments:
- snapshots: bfloat16 [131072, 512], P('rows', 'freq'), may hold values from -60 to 60
- block_cols: int32 [1024, 3], P('rows'), may hold values from 0 to 1023, as said below
- mass_blocks: bfloat16 [1024, 3, 128, 128], P('rows'), may hold values from -2 to 2
- start_group: float32 [512, 32], P('freq'), may hold values from -6 to 6
- start_merge: float32 [64, 32], replicated, may hold values from -6 to 6
Outputs:
- modes: float32 [32, 131072], P(None, ('rows', 'freq'))
The draws below stay inside these ranges and needn't reach their ends.
Inputs may be any that keep to these rules, and one draw needn't show every extreme that they name: block_cols[b, 0] is b; the other entries lie within 2 of b, differ from b, and may repeat near the ends.
All inputs are finite; a program needn't handle non-finite values.
Results may differ from the reference program's by a relative error of at most 0.0003.
Values may be sent and summed in bfloat16 or wider, within the bound.
A program may use at most 128 MiB of HBM per device.

```python
import math
import jax
import jax.numpy as jnp
from jax import lax

BLK = 128
KB = 3
HB = 2
COLS = 512
RANK = 32
POWER = 2
COLS_DEV = 128
NB = 1024
NROWS = 131072
LEVELS = 2
N_FREQ = 4


def draw_snapshots(key, part):
    basis_key, mixing_key, noise_key, column_key, row_key, wave_key, phase_key, depth_key = jax.random.split(key, 8)
    shared_rank = 64
    position = (jnp.arange(NROWS, dtype=jnp.float32) + 0.5) / NROWS
    waves = jax.random.randint(wave_key, (1, shared_rank), 1, 4).astype(jnp.float32)
    phases = jax.random.uniform(phase_key, (1, shared_rank), jnp.float32, 0.0, 2.0 * math.pi)
    depth = jax.random.uniform(depth_key, (1, shared_rank), jnp.float32, 0.3, 1.0)
    envelope = jnp.exp(depth * jnp.sin(2.0 * math.pi * waves * position[:, None] + phases))
    trend = jnp.exp(math.log(3.0) * position)[:, None]
    mode_index = jnp.arange(shared_rank, dtype=jnp.float32)
    basis = jax.random.normal(basis_key, (NROWS, shared_rank), jnp.float32)
    mixing = jax.random.normal(mixing_key, (shared_rank, COLS), jnp.float32)
    noise = jax.random.normal(noise_key, (NROWS, COLS), jnp.float32)
    decay = 1.0 / (1.0 + mode_index / 16.0)
    column_scale = jnp.exp(jax.random.uniform(column_key, (1, COLS), jnp.float32, math.log(0.3), math.log(3.0)))
    row_scale = jnp.exp(jax.random.uniform(row_key, (NROWS, 1), jnp.float32, math.log(0.5), math.log(2.0)))
    decay = decay / jnp.sqrt(jnp.sum(decay * decay))
    shared = jnp.dot(basis * envelope * decay[None, :], mixing, precision=lax.Precision.HIGHEST)
    values = 0.2 * (shared + 0.4 * noise) * column_scale * row_scale * trend
    return jnp.clip(values, -60.0, 60.0).astype(jnp.bfloat16)


def draw_block_cols(key, part):
    scores = jax.random.randint(key, (NB, 2 * HB), 0, 1 << 20) * (2 * HB) + jnp.arange(2 * HB)
    ordering = jnp.argsort(scores, axis=1)
    choices_table = jnp.concatenate([-jnp.arange(HB, 0, -1), jnp.arange(1, HB + 1)])
    offsets = choices_table[ordering[:, :KB - 1]]
    own_block = jnp.arange(NB)[:, None]
    target = own_block + offsets
    target = jnp.where((target < 0) | (target >= NB), own_block - offsets, target)
    return jnp.concatenate([own_block, target], axis=1).astype(jnp.int32)


def draw_mass_blocks(key, part):
    values = jax.random.normal(key, (NB, KB, BLK, BLK), jnp.float32)
    is_diagonal = (jnp.arange(KB) == 0)[None, :, None, None]
    spread = jnp.where(is_diagonal, 0.3, 0.5) / math.sqrt(BLK)
    identity_part = jnp.where(is_diagonal, jnp.eye(BLK, dtype=jnp.float32)[None, None], 0.0)
    return jnp.clip(identity_part + spread * values, -2.0, 2.0).astype(jnp.bfloat16)


def block_levels(stream_key, shape, shards, smallest, largest):
    def one(dim, blocks):
        steps = jax.random.uniform(jax.random.fold_in(jax.random.fold_in(stream_key, 6), dim), (blocks,), jnp.float32, smallest / len(shards), largest / len(shards))
        return jnp.repeat(jnp.exp(steps), shape[dim] // blocks).reshape((-1,) + (1,) * (len(shape) - dim - 1))

    loudness = one(*shards[0])
    for cut in shards[1:]:
        loudness = loudness * one(*cut)
    return loudness


def scatter_about(own_key, extent, scale, limit, cuts=(), kind=jnp.bfloat16):
    entries = scale * jax.random.normal(own_key, extent, jnp.float32)
    if cuts:
        entries = entries * block_levels(own_key, extent, cuts, -0.22, 0.18)
    return jnp.clip(entries, -limit, limit).astype(kind)


def setup_inputs(seed: int = 0) -> dict:
    seeds = jax.random.split(jax.random.key(seed), 6)
    return {
        "snapshots": draw_snapshots(jax.random.fold_in(seeds[5], 71), 0),
        "block_cols": draw_block_cols(jax.random.fold_in(seeds[5], 71), 0),
        "mass_blocks": draw_mass_blocks(jax.random.fold_in(seeds[5], 71), 0),
        "start_group": scatter_about(seeds[3], (COLS, RANK), 1.0, 6.0, ((0, 4),), jnp.float32),
        "start_merge": scatter_about(seeds[4], (2 * RANK, RANK), 1.0, 6.0, (), jnp.float32),
    }


HIGHEST = lax.Precision.HIGHEST

def orthonormal(columns_block):
    inner_gram = jnp.dot(columns_block.T, columns_block, precision=HIGHEST)
    lower_factor = jnp.linalg.cholesky(inner_gram)
    return lax.linalg.triangular_solve(lower_factor, columns_block, left_side=False, lower=True, transpose_a=True)

def subspace(gram_matrix, start_block):
    current = start_block
    for repeat in range(POWER):
        current = orthonormal(jnp.dot(gram_matrix, current, precision=HIGHEST))
    return current

def apply_mass(snapshots, block_cols, mass_blocks):
    padded = jnp.pad(snapshots, ((HB * BLK, HB * BLK), (0, 0)))
    tile_stack = padded.reshape(NB + 2 * HB, BLK, COLS)

    def one_row(inputs):
        columns, blocks = inputs
        picked = tile_stack[columns + HB].astype(jnp.float32)
        return jnp.einsum('kij,kjc->ic', blocks.astype(jnp.float32), picked, precision=HIGHEST)
    return lax.map(one_row, (block_cols, mass_blocks)).reshape(NB * BLK, COLS)

def reference(snapshots, block_cols, mass_blocks, start_group, start_merge):
    weighted = apply_mass(snapshots, block_cols, mass_blocks)
    nodes = []
    for group_id in range(N_FREQ):
        part_cols = weighted[:, group_id * COLS_DEV:(group_id + 1) * COLS_DEV]
        group_gram = jnp.dot(part_cols.T, part_cols, precision=HIGHEST) / NROWS
        weights = subspace(group_gram, start_group[group_id * COLS_DEV:(group_id + 1) * COLS_DEV])
        nodes.append(jnp.dot(weights.T, part_cols.T, precision=HIGHEST))
    for section_index in range(LEVELS):
        merged = []
        for position in range(0, len(nodes), 2):
            joined = jnp.concatenate([nodes[position], nodes[position + 1]], axis=0)
            pair_gram = jnp.dot(joined, joined.T, precision=HIGHEST) / NROWS
            merged.append(jnp.dot(subspace(pair_gram, start_merge).T, joined, precision=HIGHEST))
        nodes = merged
    return nodes[0]
```

```python
import functools

import jax
import jax.numpy as jnp
from jax import lax
from jax.experimental import pallas as pl
from jax.experimental.pallas import tpu as pltpu
from jax.sharding import PartitionSpec as P

HB = 2
POWER = 2
RANK = 32
LANES = 128
STEP = 4
PIECES = 4
MASS_PIECES = 4
HIGHEST = lax.Precision.HIGHEST
MESH = pl.DeviceIdType.MESH
TRANS_B = (((1,), (1,)), ((), ()))
TRANS_A = (((0,), (0,)), ((), ()))


def dot32(a, b):
    return jnp.dot(a, b, precision=HIGHEST, preferred_element_type=jnp.float32)


def dot32_tb(a, b):
    return lax.dot_general(a, b, TRANS_B, precision=HIGHEST, preferred_element_type=jnp.float32)


def split(a):
    high = a.astype(jnp.bfloat16)
    return high, (a - high.astype(jnp.float32)).astype(jnp.bfloat16)


def pad_rows(a):
    return jnp.concatenate([a, jnp.zeros((LANES - a.shape[0], a.shape[1]), a.dtype)], axis=0)


def orthonormal_all(tops):
    row = lax.broadcasted_iota(jnp.int32, (8, LANES), 0)
    lane = lax.broadcasted_iota(jnp.int32, (8, LANES), 1)
    grams = [dot32_tb(top, pad_rows(top)) for top in tops]
    nblk = RANK // 8
    left = [[g[8 * i:8 * i + 8] for i in range(nblk)] for g in grams]
    right = [[t[8 * i:8 * i + 8] for i in range(nblk)] for t in tops]
    for j in range(RANK):
        blk, sub = j // 8, j % 8
        for a, u in zip(left, right):
            pivot_a = a[blk][sub:sub + 1]
            pivot_u = u[blk][sub:sub + 1]
            inverse = 1.0 / pivot_a[:, j:j + 1]
            scaled_a = pivot_a * inverse
            scaled_u = pivot_u * inverse
            for i in range(blk, nblk):
                column = a[i][:, j:j + 1]
                if i == blk:
                    column = jnp.where(row[:, :1] > sub, column, 0.0)
                a[i] = a[i] - column * scaled_a
                u[i] = u[i] - column * scaled_u
    outs = []
    for a, u in zip(left, right):
        done = []
        for i in range(nblk):
            diagonal = jnp.sum(jnp.where(lane == row + 8 * i, a[i], 0.0), axis=1, keepdims=True)
            done.append(u[i] * lax.rsqrt(diagonal))
        outs.append(jnp.concatenate(done, axis=0))
    return outs


def subspace_all(grams, starts):
    def body(_, tops):
        return tuple(orthonormal_all([dot32(t, g()) for t, g in zip(tops, grams)]))

    return lax.fori_loop(0, POWER, body, tuple(starts))


def kernel(
    row_count, freq_count, total_rows,
    snap, cols, mass, start_group, start_merge, out,
    x0, x1, mb, wh, wl, acc, gown, gin, rs, gfull, tbuf, starts, cbuf, sbuf, dbuf, hbuf, xr, xf,
    msem, lsem, xsend, xrecv, ssem, esem, rs_s, rs_r, ag_s, ag_r, fsem, psem_s, psem_r, dsem,
    xr_s, xr_r, xf_s, xf_r,
):
    r = lax.axis_index("rows")
    f = lax.axis_index("freq")
    c = lax.rem(f, 2)
    x = f // 2
    f_pair = f + 1 - 2 * c
    f_far = lax.rem(f + 2, 4)
    chunk = x0.shape[1] - 2 * HB
    blocks = snap.shape[0]
    size = snap.shape[1]
    xs = (x0, x1)

    def dev(rr, ff):
        return {"rows": rr, "freq": ff}

    def remote(src, dst, s_sem, r_sem, rr, ff):
        return pltpu.make_async_remote_copy(
            src_ref=src, dst_ref=dst, send_sem=s_sem, recv_sem=r_sem,
            device_id=dev(rr, ff), device_id_type=MESH,
        )

    mper = chunk // MASS_PIECES

    def mass_copy(q, p):
        base = (2 * q + c) * chunk + p * mper
        return pltpu.make_async_copy(
            mass.at[pl.ds(base, mper)], mb.at[q, pl.ds(p * mper, mper)], msem.at[q, p]
        )

    def main_range(q, d):
        return pl.ds((2 * q + d) * chunk - (HB if q else 0), chunk + HB)

    def main_dst(q):
        return pl.ds(0 if q else HB, chunk + HB)

    def edge_src(q):
        return pl.ds(chunk - HB if q == 0 else 3 * chunk, HB)

    def edge_dst(q):
        return pl.ds(0 if q == 0 else chunk + HB, HB)

    local_main = [
        pltpu.make_async_copy(snap.at[main_range(q, c)], xs[q].at[c, main_dst(q)], lsem.at[q]) for q in range(2)
    ]
    local_edge = [
        pltpu.make_async_copy(snap.at[edge_src(q)], xs[q].at[c, edge_dst(q)], lsem.at[2 + q]) for q in range(2)
    ]
    inner_edge = [c == 1, c == 0]
    for q in range(2):
        local_main[q].start()
        pl.when(inner_edge[q])(local_edge[q].start)
        for p in range(MASS_PIECES):
            mass_copy(q, p).start()

    barrier = pltpu.get_barrier_semaphore()

    def greet(rr, ff):
        pl.semaphore_signal(barrier, inc=1, device_id=dev(rr, ff), device_id_type=MESH)

    @pl.loop(1, row_count)
    def _(j):
        greet(lax.rem(r + j, row_count), f)

    for j in range(1, freq_count):
        greet(r, lax.rem(f + j, freq_count))
    has_prev = r > 0
    has_next = r < row_count - 1
    pl.when(has_prev)(lambda: greet(r - 1, f_pair))
    pl.when(has_next)(lambda: greet(r + 1, f_pair))
    expected = (
        row_count - 1 + freq_count - 1 + has_prev.astype(jnp.int32) + has_next.astype(jnp.int32)
    )
    pl.semaphore_wait(barrier, expected)

    pair_main = [
        remote(snap.at[main_range(q, 1 - c)], xs[q].at[c, main_dst(q)], xsend.at[q], xrecv.at[q], r, f_pair)
        for q in range(2)
    ]
    pair_edge = [
        remote(snap.at[edge_src(q)], xs[q].at[c, edge_dst(q)], xsend.at[2 + q], xrecv.at[2 + q], r, f_pair)
        for q in range(2)
    ]
    low_f = 2 * x
    high_f = 2 * x + 1
    to_next = remote(
        snap.at[pl.ds(blocks - HB, HB)], x0.at[c, edge_dst(0)], xsend.at[4], xrecv.at[4 + c], r + 1, low_f
    )
    to_prev = remote(
        snap.at[pl.ds(0, HB)], x1.at[c, edge_dst(1)], xsend.at[5], xrecv.at[6 + c], r - 1, high_f
    )
    pl.when(has_next)(to_next.start)
    pl.when(has_prev)(to_prev.start)
    pl.when(c == 0)(pair_edge[0].start)
    pair_main[0].start()
    pl.when(c == 1)(pair_edge[1].start)
    pair_main[1].start()

    tbuf[...] = jnp.zeros_like(tbuf)
    tbuf[:, 0:RANK] = start_group[...]
    starts[c] = tbuf[...].T[0:RANK]
    start_copy = remote(starts.at[c], starts.at[c], ssem.at[0], ssem.at[1], r, f_pair)
    start_copy.start()

    acc[...] = jnp.zeros_like(acc)

    def wait_edge(q, h):
        remote(
            snap.at[pl.ds(0, HB)], xs[q].at[h, edge_dst(q)], xsend.at[4], xrecv.at[4 + 2 * q + h], r, f_pair
        ).wait_recv()

    for q in range(2):
        local_main[q].wait()
        pair_main[q].wait_recv()
        outer = c == (1 if q else 0)

        @pl.when(inner_edge[q])
        def _():
            local_edge[q].wait()
            pair_edge[q].wait_recv()

        @pl.when(jnp.logical_and(outer, has_next if q else has_prev))
        def _():
            wait_edge(q, 0)
            wait_edge(q, 1)

        first = (2 * q + c) * chunk
        for p in range(MASS_PIECES):
            mass_copy(q, p).wait()

            @pl.loop(0, mper // STEP)
            def _(t):
                rows_done = []
                for s in range(STEP):
                    b = p * mper + t * STEP + s
                    picks = []
                    for k in range(cols.shape[1]):
                        index = jnp.clip(cols[first + b, k] - r * blocks - first + HB, 0, chunk + 2 * HB - 1)
                        picks.append(jnp.concatenate([xs[q][0, index], xs[q][1, index]], axis=1))
                    factor = jnp.concatenate([mb[q, b, k] for k in range(cols.shape[1])], axis=1)
                    rows_done.append(
                        jnp.dot(factor, jnp.concatenate(picks, axis=0), preferred_element_type=jnp.float32)
                    )
                high, low = split(jnp.concatenate(rows_done, axis=0))
                where = pl.ds(pl.multiple_of((p * mper + t * STEP) * size, STEP * size), STEP * size)
                wh[q, where, :] = high
                wl[q, where, :] = low
                acc[...] += lax.dot_general(
                    high, jnp.concatenate([high, low], axis=1), TRANS_A, preferred_element_type=jnp.float32
                )

    width = 2 * size
    gown[...] = acc[:, 0:width] + 2.0 * acc[:, width:2 * width]
    mine = pl.ds(pl.multiple_of(c * size, size), size)
    other = pl.ds(pl.multiple_of((1 - c) * size, size), size)
    exchange = remote(gown.at[other], gin, esem.at[0], esem.at[1], r, f_pair)
    exchange.start()
    exchange.wait()
    gin[...] = gin[...] + gown[mine, :]
    piece = rs.shape[1]
    owners = size // piece

    def part(i):
        return pl.ds(pl.multiple_of(i * piece, piece), piece)

    def owned(i, action):
        if owners == row_count:
            action()
        else:
            pl.when(i < owners)(action)

    def rs_copy(slot, target):
        return remote(
            gin.at[part(lax.min(target, owners - 1))], rs.at[slot], rs_s.at[target], rs_r.at[slot], target, f
        )

    def summed(i):
        return gfull.at[pl.ds(pl.multiple_of(c * size + i * piece, piece), piece)]

    def ag_copy(source, target):
        return remote(summed(source), summed(source), ag_s.at[target], ag_r.at[source], target, f)

    @pl.loop(1, row_count)
    def _(j):
        target = lax.rem(r + j, row_count)
        owned(target, lambda: rs_copy(r, target).start())

    def reduce_own():
        rs[r] = gin[part(r), :]

        @pl.loop(1, row_count)
        def _(j):
            source = lax.rem(r + j, row_count)
            rs_copy(source, source).wait_recv()

        total = rs[0]
        for s in range(1, row_count):
            total = total + rs[s]
        gfull[pl.ds(pl.multiple_of(c * size + r * piece, piece), piece), :] = total

        @pl.loop(1, row_count)
        def _(j):
            ag_copy(r, lax.rem(r + j, row_count)).start()

    owned(r, reduce_own)

    @pl.loop(1, row_count)
    def _(j):
        source = lax.rem(r + j, row_count)
        owned(source, lambda: ag_copy(source, source).wait_recv())

    give = remote(gfull.at[mine], gfull.at[mine], fsem.at[0], fsem.at[1], r, f_pair)
    give.start()
    start_copy.wait()
    give.wait()

    scale = 0.5 / total_rows
    for i in range(2):
        for j in range(2):
            a = slice(i * size, (i + 1) * size)
            b = slice(j * size, (j + 1) * size)
            gown[a, b] = (gfull[a, b] + gfull[b, a].T) * scale

    s0, s1 = subspace_all(
        [lambda: gown[0:size, 0:size], lambda: gown[size:width, size:width]], [starts[0], starts[1]]
    )
    zero = jnp.zeros((RANK, size), jnp.float32)
    basis = pad_rows(
        jnp.concatenate([jnp.concatenate([s0, zero], axis=1), jnp.concatenate([zero, s1], axis=1)], axis=0)
    )
    hbuf[...] = dot32_tb(dot32(basis, gown[...]), basis)
    tbuf[...] = jnp.zeros_like(tbuf)
    tbuf[0:2 * RANK, 0:RANK] = start_merge[...]
    merge_start = tbuf[...].T[0:RANK]
    (sm,) = subspace_all([lambda: hbuf[...]], [merge_start])
    weights = dot32(sm, basis)
    th, tl = split(weights)
    both = jnp.concatenate([th, tl], axis=0)
    pair_rows = pl.ds(pl.multiple_of(x * RANK, RANK), RANK)
    span = chunk * size // PIECES

    def modes_of(q, p):
        at = pl.ds(p * span, span)
        full = lax.dot_general(both, wh[q, at, :], TRANS_B, preferred_element_type=jnp.float32)
        rest = lax.dot_general(th, wl[q, at, :], TRANS_B, preferred_element_type=jnp.float32)
        return full[0:RANK] + (full[RANK:2 * RANK] + rest)

    def far_copy(p):
        at = pl.ds(p * span, span)
        return remote(sbuf.at[:, at], cbuf.at[pair_rows, at], psem_s.at[p], psem_r.at[p], r, f_far)

    for p in range(PIECES):
        sbuf[:, p * span:(p + 1) * span] = modes_of(1 - x, p)
        far_copy(p).start()
    dbuf[x] = dot32_tb(dot32(sm, hbuf[...]), pad_rows(sm))
    diag_copy = remote(dbuf.at[x], dbuf.at[x], dsem.at[0], dsem.at[1], r, f_far)
    diag_copy.start()
    for p in range(PIECES):
        cbuf[pair_rows, p * span:(p + 1) * span] = modes_of(x, p)
    cross = jnp.zeros((RANK, LANES), jnp.float32)
    for p in range(PIECES):
        far_copy(p).wait_recv()
        at = slice(p * span, (p + 1) * span)
        ah, al = split(cbuf[0:RANK, at])
        bh, bl = split(cbuf[RANK:2 * RANK, at])
        full = lax.dot_general(
            jnp.concatenate([ah, al], axis=0), pad_rows(bh), TRANS_B, preferred_element_type=jnp.float32
        )
        rest = lax.dot_general(ah, pad_rows(bl), TRANS_B, preferred_element_type=jnp.float32)
        cross = cross + (full[0:RANK] + (full[RANK:2 * RANK] + rest))

    packed = cross[0:8]
    for i in range(1, RANK // 8):
        packed = packed + pltpu.roll(cross[8 * i:8 * i + 8], RANK * i, 1)
    xr[r] = packed

    def xr_copy(source, target):
        return remote(xr.at[source], xr.at[source], xr_s.at[target], xr_r.at[source], target, f)

    @pl.loop(1, row_count)
    def _(j):
        xr_copy(r, lax.rem(r + j, row_count)).start()

    @pl.loop(1, row_count)
    def _(j):
        source = lax.rem(r + j, row_count)
        xr_copy(source, source).wait_recv()

    total = xr[0]
    for s in range(1, row_count):
        total = total + xr[s]
    xf[f] = total

    def xf_copy(source, target):
        return remote(xf.at[source], xf.at[source], xf_s.at[target], xf_r.at[source], r, target)

    for j in range(1, freq_count):
        xf_copy(f, lax.rem(f + j, freq_count)).start()
    for j in range(1, freq_count):
        source = lax.rem(f + j, freq_count)
        xf_copy(source, source).wait_recv()
    total = xf[0]
    for s in range(1, freq_count):
        total = total + xf[s]
    total = total * (1.0 / total_rows)
    diag_copy.wait()

    lane8 = lax.broadcasted_iota(jnp.int32, (8, LANES), 1)
    crossed = pad_rows(
        jnp.concatenate(
            [
                jnp.where(lane8 < RANK, pltpu.roll(total, LANES - RANK * i, 1) if i else total, 0.0)
                for i in range(RANK // 8)
            ],
            axis=0,
        )
    )
    hbuf[...] = jnp.zeros_like(hbuf)
    hbuf[0:RANK] = dbuf[0] + pltpu.roll(crossed[0:RANK], RANK, 1)
    hbuf[RANK:2 * RANK] = crossed.T[0:RANK] + pltpu.roll(dbuf[1], RANK, 1)
    (final,) = subspace_all([lambda: hbuf[...]], [merge_start])
    fh, fl = split(final[:, 0:2 * RANK])
    fboth = jnp.concatenate([fh, fl], axis=0)
    for p in range(PIECES):
        at = slice(p * span, (p + 1) * span)
        ch, cl = split(cbuf[:, at])
        full = jnp.dot(fboth, ch, preferred_element_type=jnp.float32)
        rest = jnp.dot(fh, cl, preferred_element_type=jnp.float32)
        out[:, at] = full[0:RANK] + (full[RANK:2 * RANK] + rest)

    for q in range(2):
        pair_main[q].wait_send()
    pl.when(c == 0)(pair_edge[0].wait_send)
    pl.when(c == 1)(pair_edge[1].wait_send)
    pl.when(has_next)(to_next.wait_send)
    pl.when(has_prev)(to_prev.wait_send)
    for p in range(PIECES):
        far_copy(p).wait_send()

    @pl.loop(1, row_count)
    def _(j):
        target = lax.rem(r + j, row_count)
        owned(target, lambda: rs_copy(r, target).wait_send())
        owned(r, lambda: ag_copy(r, target).wait_send())
        xr_copy(r, target).wait_send()

    for j in range(1, freq_count):
        xf_copy(f, lax.rem(f + j, freq_count)).wait_send()


def shards(snapshots, block_cols, mass_blocks, start_group, start_merge):
    size = mass_blocks.shape[2]
    blocks = block_cols.shape[0]
    row_count = lax.axis_size("rows")
    freq_count = lax.axis_size("freq")
    chunk = blocks // freq_count
    total_rows = row_count * snapshots.shape[0]
    piece = max(size // row_count, 8)
    share = chunk * size
    f32, bf16 = jnp.float32, jnp.bfloat16
    dma = pltpu.SemaphoreType.DMA
    any_spec = pl.BlockSpec(memory_space=pl.ANY)
    vmem = pl.BlockSpec(memory_space=pltpu.VMEM)
    smem = pl.BlockSpec(memory_space=pltpu.SMEM)
    return pl.pallas_call(
        functools.partial(kernel, row_count, freq_count, total_rows),
        out_shape=jax.ShapeDtypeStruct((RANK, share), f32),
        in_specs=[any_spec, smem, any_spec, vmem, vmem],
        out_specs=vmem,
        scratch_shapes=[
            pltpu.VMEM((2, chunk + 2 * HB, size, size), bf16),
            pltpu.VMEM((2, chunk + 2 * HB, size, size), bf16),
            pltpu.VMEM((2, chunk) + mass_blocks.shape[1:], bf16),
            pltpu.VMEM((2, share, 2 * size), bf16),
            pltpu.VMEM((2, share, 2 * size), bf16),
            pltpu.VMEM((2 * size, 4 * size), f32),
            pltpu.VMEM((2 * size, 2 * size), f32),
            pltpu.VMEM((size, 2 * size), f32),
            pltpu.VMEM((row_count, piece, 2 * size), f32),
            pltpu.VMEM((2 * size, 2 * size), f32),
            pltpu.VMEM((LANES, LANES), f32),
            pltpu.VMEM((2, RANK, LANES), f32),
            pltpu.VMEM((2 * RANK, share), f32),
            pltpu.VMEM((RANK, share), f32),
            pltpu.VMEM((2, RANK, LANES), f32),
            pltpu.VMEM((LANES, LANES), f32),
            pltpu.VMEM((row_count, 8, LANES), f32),
            pltpu.VMEM((freq_count, 8, LANES), f32),
            dma((2, MASS_PIECES)),
            dma((4,)),
            dma((6,)),
            dma((8,)),
            dma((2,)),
            dma((2,)),
            dma((row_count,)),
            dma((row_count,)),
            dma((row_count,)),
            dma((row_count,)),
            dma((2,)),
            dma((PIECES,)),
            dma((PIECES,)),
            dma((2,)),
            dma((row_count,)),
            dma((row_count,)),
            dma((freq_count,)),
            dma((freq_count,)),
        ],
        compiler_params=pltpu.CompilerParams(
            collective_id=0, has_side_effects=True, vmem_limit_bytes=48 * 1024 * 1024
        ),
    )(snapshots.reshape(blocks, size, snapshots.shape[1]), block_cols, mass_blocks, start_group, start_merge)


def solution(mesh):
    in_specs = (
        P("rows", "freq"),
        P("rows", None),
        P("rows", None, None, None),
        P("freq", None),
        P(),
    )
    out_specs = P(None, ("rows", "freq"))
    return jax.shard_map(shards, mesh=mesh, in_specs=in_specs, out_specs=out_specs, check_vma=False)
```

```python
import functools

import jax
import jax.numpy as jnp
from jax import lax
from jax.experimental import pallas as pl
from jax.experimental.pallas import tpu as pltpu
from jax.sharding import PartitionSpec as P

HB = 2
POWER = 2
RANK = 32
LANES = 128
STEP = 4
GROUP = 4
PIECES = 4
FAR = 2
LEVEL = 32767.0
MASS_PIECES = 4
HIGHEST = lax.Precision.HIGHEST
MESH = pl.DeviceIdType.MESH
TRANS_B = (((1,), (1,)), ((), ()))
TRANS_A = (((0,), (0,)), ((), ()))


def dot32(a, b):
    return jnp.dot(a, b, precision=HIGHEST, preferred_element_type=jnp.float32)


def dot32_tb(a, b):
    return lax.dot_general(a, b, TRANS_B, precision=HIGHEST, preferred_element_type=jnp.float32)


def split(a):
    high = a.astype(jnp.bfloat16)
    return high, (a - high.astype(jnp.float32)).astype(jnp.bfloat16)


def pad_rows(a):
    return jnp.concatenate([a, jnp.zeros((LANES - a.shape[0], a.shape[1]), a.dtype)], axis=0)


def orthonormal_all(tops):
    row = lax.broadcasted_iota(jnp.int32, (8, LANES), 0)
    grams = [dot32_tb(top, pad_rows(top)) for top in tops]
    nblk = RANK // 8
    left = [[g[8 * i:8 * i + 8] for i in range(nblk)] for g in grams]
    right = [[t[8 * i:8 * i + 8] for i in range(nblk)] for t in tops]
    scales = [[[] for _ in range(nblk)] for _ in tops]
    for base in range(0, RANK, GROUP):
        blk = base // 8
        spread = [
            [
                [jnp.broadcast_to(a[i][:, base + k:base + k + 1], (8, LANES)) for i in range(blk, nblk)]
                for k in range(GROUP)
            ]
            for a in left
        ]
        for k in range(GROUP):
            sub = (base + k) % 8
            for n, (a, u, columns) in enumerate(zip(left, right, spread)):
                pivot = jnp.broadcast_to(columns[k][0][sub:sub + 1], (8, LANES))
                scales[n][blk].append(pivot)
                inverse = 1.0 / pivot
                factor = [column * inverse for column in columns[k]]
                factor[0] = jnp.where(row > sub, factor[0], 0.0)
                for later in range(k + 1, GROUP):
                    entry = jnp.broadcast_to(columns[later][0][sub:sub + 1], (8, LANES))
                    columns[later] = [col - m * entry for col, m in zip(columns[later], factor)]
                pivot_a = jnp.broadcast_to(a[blk][sub:sub + 1], (8, LANES))
                pivot_u = jnp.broadcast_to(u[blk][sub:sub + 1], (8, LANES))
                for i in range(blk, nblk):
                    a[i] = a[i] - factor[i - blk] * pivot_a
                    u[i] = u[i] - factor[i - blk] * pivot_u
    outs = []
    for u, pivots in zip(right, scales):
        done = []
        for i in range(nblk):
            diagonal = pivots[i][0]
            for sub in range(1, 8):
                diagonal = jnp.where(row == sub, pivots[i][sub], diagonal)
            done.append(u[i] * lax.rsqrt(diagonal))
        outs.append(jnp.concatenate(done, axis=0))
    return outs


def subspace_all(grams, starts):
    def body(_, tops):
        return tuple(orthonormal_all([dot32(t, g()) for t, g in zip(tops, grams)]))

    return lax.fori_loop(0, POWER, body, tuple(starts))


def kernel(
    row_count, freq_count, total_rows,
    snap, cols, mass, start_group, start_merge, out,
    x0, x1, mb, wh, wl, acc, gown, rs, gfull, tbuf, starts, cbuf, qsend, qrecv, ssend, srecv, dbuf, hbuf, xr, xf,
    msem, lsem, xsend, xrecv, ssem, rs_s, rs_r, ag_s, ag_r, psem_s, psem_r, dsem,
    xr_s, xr_r, xf_s, xf_r,
):
    r = lax.axis_index("rows")
    f = lax.axis_index("freq")
    c = lax.rem(f, 2)
    x = f // 2
    f_pair = f + 1 - 2 * c
    f_far = lax.rem(f + 2, 4)
    chunk = x0.shape[1] - 2 * HB
    blocks = snap.shape[0]
    size = snap.shape[1]
    xs = (x0, x1)

    def dev(rr, ff):
        return {"rows": rr, "freq": ff}

    def remote(src, dst, s_sem, r_sem, rr, ff):
        return pltpu.make_async_remote_copy(
            src_ref=src, dst_ref=dst, send_sem=s_sem, recv_sem=r_sem,
            device_id=dev(rr, ff), device_id_type=MESH,
        )

    mper = chunk // MASS_PIECES

    def mass_copy(q, p):
        base = (2 * q + c) * chunk + p * mper
        return pltpu.make_async_copy(
            mass.at[pl.ds(base, mper)], mb.at[q, pl.ds(p * mper, mper)], msem.at[q, p]
        )

    def main_range(q, d):
        return pl.ds((2 * q + d) * chunk - (HB if q else 0), chunk + HB)

    def main_dst(q):
        return pl.ds(0 if q else HB, chunk + HB)

    def edge_src(q):
        return pl.ds(chunk - HB if q == 0 else 3 * chunk, HB)

    def edge_dst(q):
        return pl.ds(0 if q == 0 else chunk + HB, HB)

    local_main = [
        pltpu.make_async_copy(snap.at[main_range(q, c)], xs[q].at[c, main_dst(q)], lsem.at[q]) for q in range(2)
    ]
    local_edge = [
        pltpu.make_async_copy(snap.at[edge_src(q)], xs[q].at[c, edge_dst(q)], lsem.at[2 + q]) for q in range(2)
    ]
    inner_edge = [c == 1, c == 0]
    for q in range(2):
        local_main[q].start()
        pl.when(inner_edge[q])(local_edge[q].start)
        for p in range(MASS_PIECES):
            mass_copy(q, p).start()

    barrier = pltpu.get_barrier_semaphore()

    def greet(rr, ff):
        pl.semaphore_signal(barrier, inc=1, device_id=dev(rr, ff), device_id_type=MESH)

    members = 2 * row_count
    me = 2 * r + c

    def member(i):
        return i // 2, 2 * x + lax.rem(i, 2)

    @pl.loop(1, members)
    def _(j):
        greet(*member(lax.rem(me + j, members)))

    greet(r, f_far)
    greet(r, lax.rem(f_pair + 2, freq_count))
    has_prev = r > 0
    has_next = r < row_count - 1
    pl.semaphore_wait(barrier, members + 1)

    pair_main = [
        remote(snap.at[main_range(q, 1 - c)], xs[q].at[c, main_dst(q)], xsend.at[q], xrecv.at[q], r, f_pair)
        for q in range(2)
    ]
    pair_edge = [
        remote(snap.at[edge_src(q)], xs[q].at[c, edge_dst(q)], xsend.at[2 + q], xrecv.at[2 + q], r, f_pair)
        for q in range(2)
    ]
    low_f = 2 * x
    high_f = 2 * x + 1
    to_next = remote(
        snap.at[pl.ds(blocks - HB, HB)], x0.at[c, edge_dst(0)], xsend.at[4], xrecv.at[4 + c], r + 1, low_f
    )
    to_prev = remote(
        snap.at[pl.ds(0, HB)], x1.at[c, edge_dst(1)], xsend.at[5], xrecv.at[6 + c], r - 1, high_f
    )
    pl.when(has_next)(to_next.start)
    pl.when(has_prev)(to_prev.start)
    pl.when(c == 0)(pair_edge[0].start)
    pair_main[0].start()
    pl.when(c == 1)(pair_edge[1].start)
    pair_main[1].start()

    starts[c] = start_group[...]
    start_copy = remote(starts.at[c], starts.at[c], ssem.at[0], ssem.at[1], r, f_pair)
    start_copy.start()

    acc[...] = jnp.zeros_like(acc)

    def wait_edge(q, h):
        remote(
            snap.at[pl.ds(0, HB)], xs[q].at[h, edge_dst(q)], xsend.at[4], xrecv.at[4 + 2 * q + h], r, f_pair
        ).wait_recv()

    for q in range(2):
        local_main[q].wait()
        pair_main[q].wait_recv()
        outer = c == (1 if q else 0)

        @pl.when(inner_edge[q])
        def _():
            local_edge[q].wait()
            pair_edge[q].wait_recv()

        @pl.when(jnp.logical_and(outer, has_next if q else has_prev))
        def _():
            wait_edge(q, 0)
            wait_edge(q, 1)

        first = (2 * q + c) * chunk
        @pl.loop(0, MASS_PIECES)
        def _(p):
            mass_copy(q, p).wait()
            for t in range(mper // STEP):
                rows_done = []
                for s in range(STEP):
                    b = p * mper + t * STEP + s
                    picks = []
                    for k in range(cols.shape[0]):
                        index = jnp.clip(cols[k, first + b] - r * blocks - first + HB, 0, chunk + 2 * HB - 1)
                        picks.append(jnp.concatenate([xs[q][0, index], xs[q][1, index]], axis=1))
                    factor = jnp.concatenate([mb[q, b, k] for k in range(cols.shape[0])], axis=1)
                    rows_done.append(
                        jnp.dot(factor, jnp.concatenate(picks, axis=0), preferred_element_type=jnp.float32)
                    )
                high, low = split(jnp.concatenate(rows_done, axis=0))
                where = pl.ds(pl.multiple_of((p * mper + t * STEP) * size, STEP * size), STEP * size)
                wh[q, where, :] = high
                wl[q, where, :] = low
                acc[...] += lax.dot_general(
                    high, jnp.concatenate([high, low], axis=1), TRANS_A, preferred_element_type=jnp.float32
                )

    width = 2 * size
    gown[...] = acc[:, 0:width] + 2.0 * acc[:, width:2 * width]
    piece = rs.shape[1]
    owners = width // piece

    def part(i):
        return pl.ds(pl.multiple_of(i * piece, piece), piece)

    def owned(i, action):
        if owners == members:
            action()
        else:
            pl.when(i < owners)(action)

    def rs_copy(slot, target):
        return remote(
            gown.at[part(lax.min(target, owners - 1))], rs.at[slot], rs_s.at[target], rs_r.at[slot], *member(target)
        )

    def ag_copy(source, target):
        at = gfull.at[part(lax.min(source, owners - 1))]
        return remote(at, at, ag_s.at[target], ag_r.at[source], *member(target))

    @pl.loop(1, members)
    def _(j):
        target = lax.rem(me + j, members)
        owned(target, lambda: rs_copy(me, target).start())

    def reduce_own():
        rs[me] = gown[part(me), :]

        @pl.loop(1, members)
        def _(j):
            source = lax.rem(me + j, members)
            rs_copy(source, source).wait_recv()

        total = rs[0]
        for s in range(1, members):
            total = total + rs[s]
        gfull[part(me), :] = total

        @pl.loop(1, members)
        def _(j):
            ag_copy(me, lax.rem(me + j, members)).start()

    owned(me, reduce_own)
    start_copy.wait()

    @pl.loop(1, members)
    def _(j):
        source = lax.rem(me + j, members)
        owned(source, lambda: ag_copy(source, source).wait_recv())
        owned(source, lambda: rs_copy(me, source).wait_send())

    scale = 0.5 / total_rows
    for i in range(2):
        for j in range(2):
            a = slice(i * size, (i + 1) * size)
            b = slice(j * size, (j + 1) * size)
            gown[a, b] = (gfull[a, b] + gfull[b, a].T) * scale

    s0, s1 = subspace_all(
        [lambda: gown[0:size, 0:size], lambda: gown[size:width, size:width]], [starts[0], starts[1]]
    )
    zero = jnp.zeros((RANK, size), jnp.float32)
    basis = pad_rows(
        jnp.concatenate([jnp.concatenate([s0, zero], axis=1), jnp.concatenate([zero, s1], axis=1)], axis=0)
    )
    hbuf[...] = dot32_tb(dot32(basis, gown[...]), basis)
    tbuf[...] = jnp.zeros_like(tbuf)
    tbuf[:, 0:2 * RANK] = start_merge[...]
    merge_start = tbuf[...]
    (sm,) = subspace_all([lambda: hbuf[...]], [merge_start])
    weights = dot32(sm, basis)
    th, tl = split(weights)
    both = jnp.concatenate([th, tl], axis=0)
    pair_rows = pl.ds(pl.multiple_of(x * RANK, RANK), RANK)
    span = chunk * size // PIECES

    def modes_of(q, p):
        at = pl.ds(p * span, span)
        full = lax.dot_general(both, wh[q, at, :], TRANS_B, preferred_element_type=jnp.float32)
        rest = lax.dot_general(th, wl[q, at, :], TRANS_B, preferred_element_type=jnp.float32)
        return full[0:RANK] + (full[RANK:2 * RANK] + rest)

    half = chunk * size // FAR
    tiles = half // LANES

    def far_copies(p):
        at = pl.ds(p * half, half)
        return (
            remote(qsend.at[:, at], qrecv.at[:, at], psem_s.at[p], psem_r.at[p], r, f_far),
            remote(ssend.at[p], srecv.at[p], psem_s.at[FAR + p], psem_r.at[FAR + p], r, f_far),
        )

    per_half = PIECES // FAR
    for p in range(FAR):
        parts = [modes_of(1 - x, p * per_half + i) for i in range(per_half)]
        cuts = [v[:, LANES * t:LANES * (t + 1)] for v in parts for t in range(span // LANES)]
        largest = jnp.full((RANK, LANES), 1e-30, jnp.float32)
        for v in cuts:
            largest = jnp.maximum(largest, jnp.abs(v))
        inverse = LEVEL / largest
        ssend[p] = largest * (1.0 / LEVEL)
        for t in range(tiles):
            at = slice(p * half + t * LANES, p * half + (t + 1) * LANES)
            qsend[:, at] = jnp.round(cuts[t] * inverse).astype(jnp.int32).astype(jnp.int16)
        for copy in far_copies(p):
            copy.start()
    dbuf[x] = dot32_tb(dot32(sm, hbuf[...]), pad_rows(sm))
    diag_copy = remote(dbuf.at[x], dbuf.at[x], dsem.at[0], dsem.at[1], r, f_far)
    diag_copy.start()
    for p in range(PIECES):
        cbuf[pair_rows, p * span:(p + 1) * span] = modes_of(x, p)
    far_rows = pl.ds(pl.multiple_of((1 - x) * RANK, RANK), RANK)
    cross = jnp.zeros((RANK, LANES), jnp.float32)
    for p in range(FAR):
        for copy in far_copies(p):
            copy.wait_recv()
        unit = srecv[p]
        for t in range(tiles):
            at = slice(p * half + t * LANES, p * half + (t + 1) * LANES)
            cbuf[far_rows, at] = qrecv[:, at].astype(jnp.int32).astype(jnp.float32) * unit
        at = slice(p * half, (p + 1) * half)
        ah, al = split(cbuf[0:RANK, at])
        bh, bl = split(cbuf[RANK:2 * RANK, at])
        full = lax.dot_general(
            jnp.concatenate([ah, al], axis=0), pad_rows(bh), TRANS_B, preferred_element_type=jnp.float32
        )
        rest = lax.dot_general(ah, pad_rows(bl), TRANS_B, preferred_element_type=jnp.float32)
        cross = cross + (full[0:RANK] + (full[RANK:2 * RANK] + rest))

    packed = cross[0:8]
    for i in range(1, RANK // 8):
        packed = packed + pltpu.roll(cross[8 * i:8 * i + 8], RANK * i, 1)
    xr[r] = packed

    def xr_copy(source, target):
        return remote(xr.at[source], xr.at[source], xr_s.at[target], xr_r.at[source], target, f)

    @pl.loop(1, row_count)
    def _(j):
        xr_copy(r, lax.rem(r + j, row_count)).start()

    @pl.loop(1, row_count)
    def _(j):
        source = lax.rem(r + j, row_count)
        xr_copy(source, source).wait_recv()

    total = xr[0]
    for s in range(1, row_count):
        total = total + xr[s]
    xf[f] = total

    def xf_copy(source, target):
        return remote(xf.at[source], xf.at[source], xf_s.at[target], xf_r.at[source], r, target)

    for j in range(1, freq_count):
        xf_copy(f, lax.rem(f + j, freq_count)).start()
    for j in range(1, freq_count):
        source = lax.rem(f + j, freq_count)
        xf_copy(source, source).wait_recv()
    total = xf[0]
    for s in range(1, freq_count):
        total = total + xf[s]
    total = total * (1.0 / total_rows)
    diag_copy.wait()

    lane8 = lax.broadcasted_iota(jnp.int32, (8, LANES), 1)
    crossed = pad_rows(
        jnp.concatenate(
            [
                jnp.where(lane8 < RANK, pltpu.roll(total, LANES - RANK * i, 1) if i else total, 0.0)
                for i in range(RANK // 8)
            ],
            axis=0,
        )
    )
    hbuf[...] = jnp.zeros_like(hbuf)
    hbuf[0:RANK] = dbuf[0] + pltpu.roll(crossed[0:RANK], RANK, 1)
    hbuf[RANK:2 * RANK] = crossed.T[0:RANK] + pltpu.roll(dbuf[1], RANK, 1)
    (final,) = subspace_all([lambda: hbuf[...]], [merge_start])
    fh, fl = split(final[:, 0:2 * RANK])
    fboth = jnp.concatenate([fh, fl], axis=0)
    for p in range(PIECES):
        at = slice(p * span, (p + 1) * span)
        ch, cl = split(cbuf[:, at])
        full = jnp.dot(fboth, ch, preferred_element_type=jnp.float32)
        rest = jnp.dot(fh, cl, preferred_element_type=jnp.float32)
        out[:, at] = full[0:RANK] + (full[RANK:2 * RANK] + rest)

    for q in range(2):
        pair_main[q].wait_send()
    pl.when(c == 0)(pair_edge[0].wait_send)
    pl.when(c == 1)(pair_edge[1].wait_send)
    pl.when(has_next)(to_next.wait_send)
    pl.when(has_prev)(to_prev.wait_send)
    for p in range(FAR):
        for copy in far_copies(p):
            copy.wait_send()

    @pl.loop(1, row_count)
    def _(j):
        xr_copy(r, lax.rem(r + j, row_count)).wait_send()

    @pl.loop(1, members)
    def _(j):
        owned(me, lambda: ag_copy(me, lax.rem(me + j, members)).wait_send())

    for j in range(1, freq_count):
        xf_copy(f, lax.rem(f + j, freq_count)).wait_send()


def shards(snapshots, block_cols, mass_blocks, start_group, start_merge):
    size = mass_blocks.shape[2]
    blocks = block_cols.shape[0]
    row_count = lax.axis_size("rows")
    freq_count = lax.axis_size("freq")
    chunk = blocks // freq_count
    total_rows = row_count * snapshots.shape[0]
    piece = max(size // row_count, 8)
    share = chunk * size
    f32, bf16 = jnp.float32, jnp.bfloat16
    dma = pltpu.SemaphoreType.DMA
    any_spec = pl.BlockSpec(memory_space=pl.ANY)
    vmem = pl.BlockSpec(memory_space=pltpu.VMEM)
    smem = pl.BlockSpec(memory_space=pltpu.SMEM)
    return pl.pallas_call(
        functools.partial(kernel, row_count, freq_count, total_rows),
        out_shape=jax.ShapeDtypeStruct((RANK, share), f32),
        in_specs=[any_spec, smem, any_spec, vmem, vmem],
        out_specs=vmem,
        scratch_shapes=[
            pltpu.VMEM((2, chunk + 2 * HB, size, size), bf16),
            pltpu.VMEM((2, chunk + 2 * HB, size, size), bf16),
            pltpu.VMEM((2, chunk) + mass_blocks.shape[1:], bf16),
            pltpu.VMEM((2, share, 2 * size), bf16),
            pltpu.VMEM((2, share, 2 * size), bf16),
            pltpu.VMEM((2 * size, 4 * size), f32),
            pltpu.VMEM((2 * size, 2 * size), f32),
            pltpu.VMEM((2 * row_count, piece, 2 * size), f32),
            pltpu.VMEM((2 * size, 2 * size), f32),
            pltpu.VMEM((RANK, LANES), f32),
            pltpu.VMEM((2, RANK, LANES), f32),
            pltpu.VMEM((2 * RANK, share), f32),
            pltpu.VMEM((RANK, share), jnp.int16),
            pltpu.VMEM((RANK, share), jnp.int16),
            pltpu.VMEM((FAR, RANK, LANES), f32),
            pltpu.VMEM((FAR, RANK, LANES), f32),
            pltpu.VMEM((2, RANK, LANES), f32),
            pltpu.VMEM((LANES, LANES), f32),
            pltpu.VMEM((row_count, 8, LANES), f32),
            pltpu.VMEM((freq_count, 8, LANES), f32),
            dma((2, MASS_PIECES)),
            dma((4,)),
            dma((6,)),
            dma((8,)),
            dma((2,)),
            dma((2 * row_count,)),
            dma((2 * row_count,)),
            dma((2 * row_count,)),
            dma((2 * row_count,)),
            dma((2 * FAR,)),
            dma((2 * FAR,)),
            dma((2,)),
            dma((row_count,)),
            dma((row_count,)),
            dma((freq_count,)),
            dma((freq_count,)),
        ],
        compiler_params=pltpu.CompilerParams(
            collective_id=0, has_side_effects=True, vmem_limit_bytes=51 * 1024 * 1024
        ),
    )(snapshots.reshape(blocks, size, snapshots.shape[1]), block_cols.T, mass_blocks, start_group.T, start_merge.T)


def solution(mesh):
    in_specs = (
        P("rows", "freq"),
        P("rows", None),
        P("rows", None, None, None),
        P("freq", None),
        P(),
    )
    out_specs = P(None, ("rows", "freq"))
    return jax.shard_map(shards, mesh=mesh, in_specs=in_specs, out_specs=out_specs, check_vma=False)
```

```python
import functools

import jax
import jax.numpy as jnp
from jax import lax
from jax.experimental import pallas as pl
from jax.experimental.pallas import tpu as pltpu
from jax.sharding import PartitionSpec as P

HB = 2
POWER = 2
RANK = 32
LANES = 128
STEP = 4
GROUP = 8
PIECES = 4
FAR = 2
LEVEL = 32767.0
MASS_PIECES = 4
HIGHEST = lax.Precision.HIGHEST
MESH = pl.DeviceIdType.MESH
TRANS_B = (((1,), (1,)), ((), ()))
TRANS_A = (((0,), (0,)), ((), ()))


def dot32(a, b):
    return jnp.dot(a, b, precision=HIGHEST, preferred_element_type=jnp.float32)


def dot32_tb(a, b):
    return lax.dot_general(a, b, TRANS_B, precision=HIGHEST, preferred_element_type=jnp.float32)


def split(a):
    high = a.astype(jnp.bfloat16)
    return high, (a - high.astype(jnp.float32)).astype(jnp.bfloat16)


def pad_rows(a):
    return jnp.concatenate([a, jnp.zeros((LANES - a.shape[0], a.shape[1]), a.dtype)], axis=0)


def orthonormal_all(tops):
    row = lax.broadcasted_iota(jnp.int32, (8, LANES), 0)
    grams = [dot32_tb(top, pad_rows(top)) for top in tops]
    nblk = RANK // 8
    left = [[g[8 * i:8 * i + 8] for i in range(nblk)] for g in grams]
    right = [[t[8 * i:8 * i + 8] for i in range(nblk)] for t in tops]
    scales = [[[] for _ in range(nblk)] for _ in tops]
    for base in range(0, RANK, GROUP):
        blk = base // 8
        spread = [
            [
                [jnp.broadcast_to(a[i][:, base + k:base + k + 1], (8, LANES)) for i in range(blk, nblk)]
                for k in range(GROUP)
            ]
            for a in left
        ]
        for k in range(GROUP):
            sub = (base + k) % 8
            for n, (a, u, columns) in enumerate(zip(left, right, spread)):
                pivot = jnp.broadcast_to(columns[k][0][sub:sub + 1], (8, LANES))
                scales[n][blk].append(pivot)
                inverse = 1.0 / pivot
                factor = [column * inverse for column in columns[k]]
                factor[0] = jnp.where(row > sub, factor[0], 0.0)
                for later in range(k + 1, GROUP):
                    entry = jnp.broadcast_to(columns[later][0][sub:sub + 1], (8, LANES))
                    columns[later] = [col - m * entry for col, m in zip(columns[later], factor)]
                pivot_a = jnp.broadcast_to(a[blk][sub:sub + 1], (8, LANES))
                pivot_u = jnp.broadcast_to(u[blk][sub:sub + 1], (8, LANES))
                for i in range(blk, nblk):
                    a[i] = a[i] - factor[i - blk] * pivot_a
                    u[i] = u[i] - factor[i - blk] * pivot_u
    outs = []
    for u, pivots in zip(right, scales):
        done = []
        for i in range(nblk):
            diagonal = pivots[i][0]
            for sub in range(1, 8):
                diagonal = jnp.where(row == sub, pivots[i][sub], diagonal)
            done.append(u[i] * lax.rsqrt(diagonal))
        outs.append(jnp.concatenate(done, axis=0))
    return outs


def subspace_all(grams, starts):
    def body(_, tops):
        return tuple(orthonormal_all([dot32(t, g()) for t, g in zip(tops, grams)]))

    return lax.fori_loop(0, POWER, body, tuple(starts))


def kernel(
    row_count, freq_count, total_rows,
    snap, cols, mass, start_group, start_merge, out,
    x0, x1, mb, wh, wl, acc, gown, rs, gfull, tbuf, starts, cbuf, qsend, qrecv, ssend, srecv, dbuf, hbuf, xr, xf,
    msem, lsem, xsend, xrecv, ssem, rs_s, rs_r, ag_s, ag_r, psem_s, psem_r, dsem,
    xr_s, xr_r, xf_s, xf_r,
):
    r = lax.axis_index("rows")
    f = lax.axis_index("freq")
    c = lax.rem(f, 2)
    x = f // 2
    f_pair = f + 1 - 2 * c
    f_far = lax.rem(f + 2, 4)
    chunk = x0.shape[1] - 2 * HB
    blocks = snap.shape[0]
    size = snap.shape[1]
    xs = (x0, x1)

    def dev(rr, ff):
        return {"rows": rr, "freq": ff}

    def remote(src, dst, s_sem, r_sem, rr, ff):
        return pltpu.make_async_remote_copy(
            src_ref=src, dst_ref=dst, send_sem=s_sem, recv_sem=r_sem,
            device_id=dev(rr, ff), device_id_type=MESH,
        )

    mper = chunk // MASS_PIECES

    def mass_copy(q, p):
        base = (2 * q + c) * chunk + p * mper
        return pltpu.make_async_copy(
            mass.at[pl.ds(base, mper)], mb.at[q, pl.ds(p * mper, mper)], msem.at[q, p]
        )

    def main_range(q, d):
        return pl.ds((2 * q + d) * chunk - (HB if q else 0), chunk + HB)

    def main_dst(q):
        return pl.ds(0 if q else HB, chunk + HB)

    def edge_src(q):
        return pl.ds(chunk - HB if q == 0 else 3 * chunk, HB)

    def edge_dst(q):
        return pl.ds(0 if q == 0 else chunk + HB, HB)

    local_main = [
        pltpu.make_async_copy(snap.at[main_range(q, c)], xs[q].at[c, main_dst(q)], lsem.at[q]) for q in range(2)
    ]
    local_edge = [
        pltpu.make_async_copy(snap.at[edge_src(q)], xs[q].at[c, edge_dst(q)], lsem.at[2 + q]) for q in range(2)
    ]
    inner_edge = [c == 1, c == 0]
    for q in range(2):
        local_main[q].start()
        pl.when(inner_edge[q])(local_edge[q].start)
        for p in range(MASS_PIECES):
            mass_copy(q, p).start()

    barrier = pltpu.get_barrier_semaphore()

    def greet(rr, ff):
        pl.semaphore_signal(barrier, inc=1, device_id=dev(rr, ff), device_id_type=MESH)

    members = 2 * row_count
    me = 2 * r + c

    def member(i):
        return i // 2, 2 * x + lax.rem(i, 2)

    @pl.loop(1, members)
    def _(j):
        greet(*member(lax.rem(me + j, members)))

    greet(r, f_far)
    greet(r, lax.rem(f_pair + 2, freq_count))
    has_prev = r > 0
    has_next = r < row_count - 1
    pl.semaphore_wait(barrier, members + 1)

    pair_main = [
        remote(snap.at[main_range(q, 1 - c)], xs[q].at[c, main_dst(q)], xsend.at[q], xrecv.at[q], r, f_pair)
        for q in range(2)
    ]
    pair_edge = [
        remote(snap.at[edge_src(q)], xs[q].at[c, edge_dst(q)], xsend.at[2 + q], xrecv.at[2 + q], r, f_pair)
        for q in range(2)
    ]
    low_f = 2 * x
    high_f = 2 * x + 1
    to_next = remote(
        snap.at[pl.ds(blocks - HB, HB)], x0.at[c, edge_dst(0)], xsend.at[4], xrecv.at[4 + c], r + 1, low_f
    )
    to_prev = remote(
        snap.at[pl.ds(0, HB)], x1.at[c, edge_dst(1)], xsend.at[5], xrecv.at[6 + c], r - 1, high_f
    )
    pl.when(has_next)(to_next.start)
    pl.when(has_prev)(to_prev.start)
    pl.when(c == 0)(pair_edge[0].start)
    pair_main[0].start()
    pl.when(c == 1)(pair_edge[1].start)
    pair_main[1].start()

    starts[c] = start_group[...]
    start_copy = remote(starts.at[c], starts.at[c], ssem.at[0], ssem.at[1], r, f_pair)
    start_copy.start()

    acc[...] = jnp.zeros_like(acc)

    def wait_edge(q, h):
        remote(
            snap.at[pl.ds(0, HB)], xs[q].at[h, edge_dst(q)], xsend.at[4], xrecv.at[4 + 2 * q + h], r, f_pair
        ).wait_recv()

    for q in range(2):
        local_main[q].wait()
        pair_main[q].wait_recv()
        outer = c == (1 if q else 0)

        @pl.when(inner_edge[q])
        def _():
            local_edge[q].wait()
            pair_edge[q].wait_recv()

        @pl.when(jnp.logical_and(outer, has_next if q else has_prev))
        def _():
            wait_edge(q, 0)
            wait_edge(q, 1)

        first = (2 * q + c) * chunk
        @pl.loop(0, MASS_PIECES)
        def _(p):
            mass_copy(q, p).wait()
            for t in range(mper // STEP):
                rows_done = []
                for s in range(STEP):
                    b = p * mper + t * STEP + s
                    picks = []
                    for k in range(cols.shape[0]):
                        index = jnp.clip(cols[k, first + b] - r * blocks - first + HB, 0, chunk + 2 * HB - 1)
                        picks.append(jnp.concatenate([xs[q][0, index], xs[q][1, index]], axis=1))
                    factor = jnp.concatenate([mb[q, b, k] for k in range(cols.shape[0])], axis=1)
                    rows_done.append(
                        jnp.dot(factor, jnp.concatenate(picks, axis=0), preferred_element_type=jnp.float32)
                    )
                high, low = split(jnp.concatenate(rows_done, axis=0))
                where = pl.ds(pl.multiple_of((p * mper + t * STEP) * size, STEP * size), STEP * size)
                wh[q, where, :] = high
                wl[q, where, :] = low
                acc[...] += lax.dot_general(
                    high, jnp.concatenate([high, low], axis=1), TRANS_A, preferred_element_type=jnp.float32
                )

    width = 2 * size
    gown[...] = acc[:, 0:width] + 2.0 * acc[:, width:2 * width]
    piece = rs.shape[1]
    owners = width // piece

    def part(i):
        return pl.ds(pl.multiple_of(i * piece, piece), piece)

    def owned(i, action):
        if owners == members:
            action()
        else:
            pl.when(i < owners)(action)

    def rs_copy(slot, target):
        return remote(
            gown.at[part(lax.min(target, owners - 1))], rs.at[slot], rs_s.at[target], rs_r.at[slot], *member(target)
        )

    def ag_copy(source, target):
        at = gfull.at[part(lax.min(source, owners - 1))]
        return remote(at, at, ag_s.at[target], ag_r.at[source], *member(target))

    @pl.loop(1, members)
    def _(j):
        target = lax.rem(me + j, members)
        owned(target, lambda: rs_copy(me, target).start())

    def reduce_own():
        rs[me] = gown[part(me), :]

        @pl.loop(1, members)
        def _(j):
            source = lax.rem(me + j, members)
            rs_copy(source, source).wait_recv()

        total = rs[0]
        for s in range(1, members):
            total = total + rs[s]
        gfull[part(me), :] = total

        @pl.loop(1, members)
        def _(j):
            ag_copy(me, lax.rem(me + j, members)).start()

    owned(me, reduce_own)
    start_copy.wait()

    @pl.loop(1, members)
    def _(j):
        source = lax.rem(me + j, members)
        owned(source, lambda: ag_copy(source, source).wait_recv())
        owned(source, lambda: rs_copy(me, source).wait_send())

    scale = 0.5 / total_rows
    for i in range(2):
        for j in range(2):
            a = slice(i * size, (i + 1) * size)
            b = slice(j * size, (j + 1) * size)
            gown[a, b] = (gfull[a, b] + gfull[b, a].T) * scale

    s0, s1 = subspace_all(
        [lambda: gown[0:size, 0:size], lambda: gown[size:width, size:width]], [starts[0], starts[1]]
    )
    zero = jnp.zeros((RANK, size), jnp.float32)
    basis = pad_rows(
        jnp.concatenate([jnp.concatenate([s0, zero], axis=1), jnp.concatenate([zero, s1], axis=1)], axis=0)
    )
    hbuf[...] = dot32_tb(dot32(basis, gown[...]), basis)
    tbuf[...] = jnp.zeros_like(tbuf)
    tbuf[:, 0:2 * RANK] = start_merge[...]
    merge_start = tbuf[...]
    (sm,) = subspace_all([lambda: hbuf[...]], [merge_start])
    weights = dot32(sm, basis)
    th, tl = split(weights)
    both = jnp.concatenate([th, tl], axis=0)
    pair_rows = pl.ds(pl.multiple_of(x * RANK, RANK), RANK)
    span = chunk * size // PIECES

    def modes_of(q, p):
        at = pl.ds(p * span, span)
        full = lax.dot_general(both, wh[q, at, :], TRANS_B, preferred_element_type=jnp.float32)
        rest = lax.dot_general(th, wl[q, at, :], TRANS_B, preferred_element_type=jnp.float32)
        return full[0:RANK] + (full[RANK:2 * RANK] + rest)

    half = chunk * size // FAR
    tiles = half // LANES

    def far_copies(p):
        at = pl.ds(p * half, half)
        return (
            remote(qsend.at[:, at], qrecv.at[:, at], psem_s.at[p], psem_r.at[p], r, f_far),
            remote(ssend.at[p], srecv.at[p], psem_s.at[FAR + p], psem_r.at[FAR + p], r, f_far),
        )

    per_half = PIECES // FAR
    for p in range(FAR):
        parts = [modes_of(1 - x, p * per_half + i) for i in range(per_half)]
        cuts = [v[:, LANES * t:LANES * (t + 1)] for v in parts for t in range(span // LANES)]
        largest = jnp.full((RANK, LANES), 1e-30, jnp.float32)
        for v in cuts:
            largest = jnp.maximum(largest, jnp.abs(v))
        inverse = LEVEL / largest
        ssend[p] = largest * (1.0 / LEVEL)
        for t in range(tiles):
            at = slice(p * half + t * LANES, p * half + (t + 1) * LANES)
            qsend[:, at] = jnp.round(cuts[t] * inverse).astype(jnp.int32).astype(jnp.int16)
        for copy in far_copies(p):
            copy.start()
    dbuf[x] = dot32_tb(dot32(sm, hbuf[...]), pad_rows(sm))
    diag_copy = remote(dbuf.at[x], dbuf.at[x], dsem.at[0], dsem.at[1], r, f_far)
    diag_copy.start()
    for p in range(PIECES):
        cbuf[pair_rows, p * span:(p + 1) * span] = modes_of(x, p)
    far_rows = pl.ds(pl.multiple_of((1 - x) * RANK, RANK), RANK)
    cross = jnp.zeros((RANK, LANES), jnp.float32)
    for p in range(FAR):
        for copy in far_copies(p):
            copy.wait_recv()
        unit = srecv[p]
        for t in range(tiles):
            at = slice(p * half + t * LANES, p * half + (t + 1) * LANES)
            cbuf[far_rows, at] = qrecv[:, at].astype(jnp.int32).astype(jnp.float32) * unit
        at = slice(p * half, (p + 1) * half)
        ah, al = split(cbuf[0:RANK, at])
        bh, bl = split(cbuf[RANK:2 * RANK, at])
        full = lax.dot_general(
            jnp.concatenate([ah, al], axis=0), pad_rows(bh), TRANS_B, preferred_element_type=jnp.float32
        )
        rest = lax.dot_general(ah, pad_rows(bl), TRANS_B, preferred_element_type=jnp.float32)
        cross = cross + (full[0:RANK] + (full[RANK:2 * RANK] + rest))

    packed = cross[0:8]
    for i in range(1, RANK // 8):
        packed = packed + pltpu.roll(cross[8 * i:8 * i + 8], RANK * i, 1)
    xr[r] = packed

    def xr_copy(source, target):
        return remote(xr.at[source], xr.at[source], xr_s.at[target], xr_r.at[source], target, f)

    @pl.loop(1, row_count)
    def _(j):
        xr_copy(r, lax.rem(r + j, row_count)).start()

    @pl.loop(1, row_count)
    def _(j):
        source = lax.rem(r + j, row_count)
        xr_copy(source, source).wait_recv()

    total = xr[0]
    for s in range(1, row_count):
        total = total + xr[s]
    xf[f] = total

    def xf_copy(source, target):
        return remote(xf.at[source], xf.at[source], xf_s.at[target], xf_r.at[source], r, target)

    for j in range(1, freq_count):
        xf_copy(f, lax.rem(f + j, freq_count)).start()
    for j in range(1, freq_count):
        source = lax.rem(f + j, freq_count)
        xf_copy(source, source).wait_recv()
    total = xf[0]
    for s in range(1, freq_count):
        total = total + xf[s]
    total = total * (1.0 / total_rows)
    diag_copy.wait()

    lane8 = lax.broadcasted_iota(jnp.int32, (8, LANES), 1)
    crossed = pad_rows(
        jnp.concatenate(
            [
                jnp.where(lane8 < RANK, pltpu.roll(total, LANES - RANK * i, 1) if i else total, 0.0)
                for i in range(RANK // 8)
            ],
            axis=0,
        )
    )
    hbuf[...] = jnp.zeros_like(hbuf)
    hbuf[0:RANK] = dbuf[0] + pltpu.roll(crossed[0:RANK], RANK, 1)
    hbuf[RANK:2 * RANK] = crossed.T[0:RANK] + pltpu.roll(dbuf[1], RANK, 1)
    (final,) = subspace_all([lambda: hbuf[...]], [merge_start])
    fh, fl = split(final[:, 0:2 * RANK])
    fboth = jnp.concatenate([fh, fl], axis=0)
    for p in range(PIECES):
        at = slice(p * span, (p + 1) * span)
        ch, cl = split(cbuf[:, at])
        full = jnp.dot(fboth, ch, preferred_element_type=jnp.float32)
        rest = jnp.dot(fh, cl, preferred_element_type=jnp.float32)
        out[:, at] = full[0:RANK] + (full[RANK:2 * RANK] + rest)

    for q in range(2):
        pair_main[q].wait_send()
    pl.when(c == 0)(pair_edge[0].wait_send)
    pl.when(c == 1)(pair_edge[1].wait_send)
    pl.when(has_next)(to_next.wait_send)
    pl.when(has_prev)(to_prev.wait_send)
    for p in range(FAR):
        for copy in far_copies(p):
            copy.wait_send()

    @pl.loop(1, row_count)
    def _(j):
        xr_copy(r, lax.rem(r + j, row_count)).wait_send()

    @pl.loop(1, members)
    def _(j):
        owned(me, lambda: ag_copy(me, lax.rem(me + j, members)).wait_send())

    for j in range(1, freq_count):
        xf_copy(f, lax.rem(f + j, freq_count)).wait_send()


def shards(snapshots, block_cols, mass_blocks, start_group, start_merge):
    size = mass_blocks.shape[2]
    blocks = block_cols.shape[0]
    row_count = lax.axis_size("rows")
    freq_count = lax.axis_size("freq")
    chunk = blocks // freq_count
    total_rows = row_count * snapshots.shape[0]
    piece = max(size // row_count, 8)
    share = chunk * size
    f32, bf16 = jnp.float32, jnp.bfloat16
    dma = pltpu.SemaphoreType.DMA
    any_spec = pl.BlockSpec(memory_space=pl.ANY)
    vmem = pl.BlockSpec(memory_space=pltpu.VMEM)
    smem = pl.BlockSpec(memory_space=pltpu.SMEM)
    return pl.pallas_call(
        functools.partial(kernel, row_count, freq_count, total_rows),
        out_shape=jax.ShapeDtypeStruct((RANK, share), f32),
        in_specs=[any_spec, smem, any_spec, vmem, vmem],
        out_specs=vmem,
        scratch_shapes=[
            pltpu.VMEM((2, chunk + 2 * HB, size, size), bf16),
            pltpu.VMEM((2, chunk + 2 * HB, size, size), bf16),
            pltpu.VMEM((2, chunk) + mass_blocks.shape[1:], bf16),
            pltpu.VMEM((2, share, 2 * size), bf16),
            pltpu.VMEM((2, share, 2 * size), bf16),
            pltpu.VMEM((2 * size, 4 * size), f32),
            pltpu.VMEM((2 * size, 2 * size), f32),
            pltpu.VMEM((2 * row_count, piece, 2 * size), f32),
            pltpu.VMEM((2 * size, 2 * size), f32),
            pltpu.VMEM((RANK, LANES), f32),
            pltpu.VMEM((2, RANK, LANES), f32),
            pltpu.VMEM((2 * RANK, share), f32),
            pltpu.VMEM((RANK, share), jnp.int16),
            pltpu.VMEM((RANK, share), jnp.int16),
            pltpu.VMEM((FAR, RANK, LANES), f32),
            pltpu.VMEM((FAR, RANK, LANES), f32),
            pltpu.VMEM((2, RANK, LANES), f32),
            pltpu.VMEM((LANES, LANES), f32),
            pltpu.VMEM((row_count, 8, LANES), f32),
            pltpu.VMEM((freq_count, 8, LANES), f32),
            dma((2, MASS_PIECES)),
            dma((4,)),
            dma((6,)),
            dma((8,)),
            dma((2,)),
            dma((2 * row_count,)),
            dma((2 * row_count,)),
            dma((2 * row_count,)),
            dma((2 * row_count,)),
            dma((2 * FAR,)),
            dma((2 * FAR,)),
            dma((2,)),
            dma((row_count,)),
            dma((row_count,)),
            dma((freq_count,)),
            dma((freq_count,)),
        ],
        compiler_params=pltpu.CompilerParams(
            collective_id=0, has_side_effects=True, vmem_limit_bytes=56 * 1024 * 1024
        ),
    )(snapshots.reshape(blocks, size, snapshots.shape[1]), block_cols.T, mass_blocks, start_group.T, start_merge.T)


def solution(mesh):
    in_specs = (
        P("rows", "freq"),
        P("rows", None),
        P("rows", None, None, None),
        P("freq", None),
        P(),
    )
    out_specs = P(None, ("rows", "freq"))
    return jax.shard_map(shards, mesh=mesh, in_specs=in_specs, out_specs=out_specs, check_vma=False)
```
